256 devices in a mesh: slab: 64 (over z, y, x_hi), quad: 4 (over x_lo, core).
Axes of the slice: x: 4 (x_hi: 2, x_lo: 2; x = x_hi * 2 + x_lo), y: 4, z: 8, core: 2. Of those that a mesh axis runs over, the one named last changes fastest.
Arguments:
- rhs: float32 [64, 4, 4, 192, 256], P('slab', 'quad'), may hold values from -6 to 6
- blocks: bfloat16 [64, 4, 4, 26, 192, 192], P('slab', 'quad'), may hold values from -0.03125 to 0.03125
- diag_blocks: bfloat16 [64, 4, 4, 192, 192], P('slab', 'quad'), may hold values from -0.2 to 1.2
- neighbours: int32 [64, 4, 4, 26], P('slab', 'quad'), may hold values from 0 to 25, each once within a row
- bound: float32 [1], replicated, may hold values from 1.9 to 2.6
- restrict_blocks: bfloat16 [8, 192, 192], replicated, may hold values from -0.21875 to 0.21875
- restrict_kind: int32 [64, 4, 4], P('slab', 'quad'), may hold values from 0 to 7
Outputs:
- smoothed: float32 [64, 4, 4, 192, 256], P('slab', 'quad')
- coarse: float32 [64, 4, 1, 192, 256], P('slab', 'quad')
The draws below stay inside these ranges and needn't reach their ends.
Inputs may be any that keep to these rules, and one draw needn't show every extreme that they name: `neighbours`: each block row names each of its 26 neighbour offsets once.
All inputs are finite; a program needn't handle non-finite values.
Results may differ from the reference program's by a relative error of at most 0.0074.
Values may be sent and summed in bfloat16 or wider, within the bound.
A program may use at most 128 MiB of HBM per device.

```python
import math
import jax
import jax.numpy as jnp
from jax import lax

BLOCK = 192
SLOTS = 26
KINDS = 8
XB = 4
NRHS = 256
Z_LAYERS = 64
Y_ROWS = 4


def draw_diag_blocks(key, part):
    shape = (Z_LAYERS, Y_ROWS, XB, BLOCK, BLOCK)
    spread = 0.2 / math.sqrt(BLOCK)
    noise = jax.random.normal(key, shape, jnp.float32) * spread
    return (noise + jnp.eye(BLOCK, dtype=jnp.float32)).astype(jnp.bfloat16)


def with_ends(result, stream_key, smallest, high):
    longest = result.shape.index(max(result.shape))
    spots = []
    for shift in (0, 1):
        where = [jax.random.randint(jax.random.fold_in(stream_key, axis), (), 0, length) for axis, length in enumerate(result.shape)]
        where[longest] = (where[longest] + shift) % result.shape[longest]
        spots.append(tuple(where))
    return result.at[spots[0]].set(smallest).at[spots[1]].set(high)


def level_of(stream_key, dims, pieces, least, high):
    def one(dim, parts):
        steps = jax.random.uniform(jax.random.fold_in(jax.random.fold_in(stream_key, 6), dim), (parts,), jnp.float32, least / len(pieces), high / len(pieces))
        return jnp.repeat(jnp.exp(steps), dims[dim] // parts).reshape((-1,) + (1,) * (len(dims) - dim - 1))

    loudness = one(*pieces[0])
    for cut in pieces[1:]:
        loudness = loudness * one(*cut)
    return loudness


def gaussian(rng, shape, scale, most, split=(), kind=jnp.bfloat16):
    entries = scale * jax.random.normal(rng, shape, jnp.float32)
    if split:
        entries = entries * level_of(rng, shape, split, -0.22, 0.18)
    return jnp.clip(entries, -most, most).astype(kind)


def setup_inputs(seed: int = 0) -> dict:
    arg_keys = jax.random.split(jax.random.key(seed), 8)
    return {
        "rhs": gaussian(arg_keys[0], (Z_LAYERS, Y_ROWS, XB, BLOCK, NRHS), 1.0, 6.0, ((0, 64), (1, 4)), jnp.float32),
        "blocks": gaussian(arg_keys[1], (Z_LAYERS, Y_ROWS, XB, SLOTS, BLOCK, BLOCK), (160 * BLOCK) ** -0.5, 0.03125, ((0, 64), (1, 4))),
        "diag_blocks": draw_diag_blocks(jax.random.fold_in(arg_keys[7], 71), 0),
        "neighbours": jax.vmap(lambda own: jax.random.permutation(own, SLOTS))(jax.random.split(arg_keys[3], Z_LAYERS * Y_ROWS * XB)).reshape((Z_LAYERS, Y_ROWS, XB, SLOTS)).astype(jnp.int32),
        "bound": jnp.clip(jax.random.uniform(arg_keys[4], (1,), jnp.float32, 1.9, 2.6), 1.9, 2.6),
        "restrict_blocks": gaussian(arg_keys[5], (KINDS, BLOCK, BLOCK), (4 * BLOCK) ** -0.5, 0.21875),
        "restrict_kind": with_ends(jax.random.randint(arg_keys[6], (Z_LAYERS, Y_ROWS, XB), 0, KINDS), jax.random.fold_in(arg_keys[6], 1), 0, KINDS - 1).astype(jnp.int32),
    }


def offsets_of(neighbours):
    offset = neighbours + (neighbours >= 13).astype(jnp.int32)
    return offset // 9, (offset // 3) % 3, offset % 3


def apply_global(vector_bf, diag_blocks, blocks, neighbours):
    layers = vector_bf.shape[0]
    rows_y = vector_bf.shape[1]
    rows_x = vector_bf.shape[2]
    padded = jnp.pad(vector_bf, ((1, 1), (1, 1), (1, 1), (0, 0), (0, 0)))
    depth_off, row_off, col_off = offsets_of(neighbours)
    ypos = jnp.arange(rows_y, dtype=jnp.int32)[None, :, None, None]
    xpos = jnp.arange(rows_x, dtype=jnp.int32)[None, None, :, None]
    flat_index = depth_off * ((rows_y + 2) * (rows_x + 2)) + (ypos + row_off) * (rows_x + 2) + xpos + col_off

    def layer(inputs):
        level, block_layer, diag_layer, index_layer = inputs
        window = lax.dynamic_slice_in_dim(padded, level, 3, 0)
        flat = window.reshape((-1,) + window.shape[3:])
        gathered = flat[index_layer]
        own = lax.dynamic_index_in_dim(vector_bf, level, 0, keepdims=False)
        image = jnp.einsum("yxsij,yxsjn->yxin", block_layer.astype(jnp.float32), gathered.astype(jnp.float32), precision=lax.Precision.HIGHEST)
        return image + jnp.einsum("yxij,yxjn->yxin", diag_layer.astype(jnp.float32), own.astype(jnp.float32), precision=lax.Precision.HIGHEST)

    return lax.map(layer, (jnp.arange(layers, dtype=jnp.int32), blocks, diag_blocks, flat_index))


def reference(rhs, blocks, diag_blocks, neighbours, bound, restrict_blocks, restrict_kind):
    theta = 9.0 * bound[0] / 16.0
    delta = 7.0 * bound[0] / 16.0
    sigma = 9.0 / 7.0
    rho_prev = 1.0 / sigma
    residual = rhs
    direction = residual / theta
    smoothed = direction
    for section in range(3):
        image = apply_global(direction.astype(jnp.bfloat16), diag_blocks, blocks, neighbours)
        residual = residual - image
        if section < 2:
            rho_next = 1.0 / (2.0 * sigma - rho_prev)
            direction = (rho_next * rho_prev) * direction + (2.0 * rho_next / delta) * residual
            smoothed = smoothed + direction
            rho_prev = rho_next
    fine = residual.astype(jnp.bfloat16)

    def restrict_layer(inputs):
        kinds, fine_layer = inputs
        chosen = restrict_blocks[kinds]
        return jnp.einsum("yxij,yxjn->yxin", chosen.astype(jnp.float32), fine_layer.astype(jnp.float32), precision=lax.Precision.HIGHEST)

    terms = lax.map(restrict_layer, (restrict_kind, fine))
    layers, rows_y, rows_x, width, count = terms.shape
    paired = terms.reshape(layers // 2, 2, rows_y, rows_x // 4, 2, 2, width, count).sum(axis=(1, 5))
    coarse = jnp.moveaxis(paired, 3, 1).reshape(layers, rows_y, rows_x // 4, width, count)
    return smoothed, coarse
```

```python
import functools

import jax
import jax.numpy as jnp
from jax import lax
from jax.experimental import pallas as pl
from jax.experimental.pallas import tpu as pltpu
from jax.sharding import PartitionSpec as P

OWN, NEAR, FAR = 0, 1, 2
SELF, SIB, CROSS = 0, 1, 2
ROUNDS = 3
HALVES = 2
MESH = pl.DeviceIdType.MESH
F32 = jnp.float32
BF16 = jnp.bfloat16


def smooth_kernel(
    layers,
    slot_ref,
    kind_ref,
    bound_ref,
    rhs_hbm,
    blocks_hbm,
    diag_hbm,
    restrict_hbm,
    smoothed_hbm,
    coarse_hbm,
    oper,
    halo,
    residual,
    direction,
    smoothed,
    restrict,
    kept,
    leaving,
    arrived,
    load_sem,
    send_sem,
    recv_sem,
    coarse_sem,
):
    s = lax.axis_index("slab")
    q = lax.axis_index("quad")
    parity = lax.rem(s, 2)
    inner = (q == 1) | (q == 2)
    near_s = s + 1 - 2 * parity
    step = 2 - 4 * parity
    sibling = (s, q + 1 - 2 * lax.rem(q, 2))
    across = (s, 3 - q)
    diagonal = (near_s, 3 - q)
    opposite = (near_s, q)
    ahead = (lax.rem(s + step + layers, layers), q)
    behind = (lax.rem(s - step + layers, layers), q)
    dz_near = 2 - 2 * parity
    dy_sib = 2 - 2 * lax.rem(q, 2)
    has_far = jnp.where(parity == 0, s > 0, s < layers - 1)
    xb, width, cols = residual.shape
    half = cols // HALVES
    slots = blocks_hbm.shape[1]

    load_rhs = pltpu.make_async_copy(rhs_hbm, residual, load_sem.at[0])
    load_diag = pltpu.make_async_copy(diag_hbm, oper.at[:, slots], load_sem.at[1])
    load_blocks = [
        pltpu.make_async_copy(blocks_hbm.at[x], oper.at[x, pl.ds(0, slots)], load_sem.at[2 + x]) for x in range(xb)
    ]
    load_restrict = pltpu.make_async_copy(restrict_hbm, restrict, load_sem.at[2 + xb])
    load_rhs.start()
    load_diag.start()
    for load in load_blocks:
        load.start()
    load_restrict.start()

    def copy(k, h, r, lane, src, dst, device):
        return pltpu.make_async_remote_copy(
            src_ref=halo.at[r, h, src[0], src[1]],
            dst_ref=halo.at[r, h, dst[0], dst[1]],
            send_sem=send_sem.at[r, h, lane],
            recv_sem=recv_sem.at[r, h, dst[0] * 3 + dst[1]],
            device_id=device,
            device_id_type=MESH,
        )

    def own_to_sib(r, h):
        return copy(0, h, r, 0, (OWN, SELF), (OWN, SIB), sibling)

    def own_to_across(r, h):
        return copy(0, h, r, 1, (OWN, SELF), (OWN, CROSS), across)

    def own_to_diagonal(r, h):
        return copy(0, h, r, 2, (OWN, SELF), (NEAR, CROSS), diagonal)

    def relay(r, h):
        if h == 0:
            return copy(0, h, r, 3, (OWN, CROSS), (NEAR, SELF), diagonal)
        return copy(0, h, r, 3, (NEAR, CROSS), (NEAR, SELF), across)

    def near_to_sib(r, h):
        return copy(0, h, r, 4, (NEAR, SELF), (NEAR, SIB), sibling)

    def near_to_ahead(r, h):
        return copy(0, h, r, 5, (NEAR, SELF), (FAR, SELF), ahead)

    def cross_to_ahead(r, h):
        return copy(0, h, r, 6, (NEAR, CROSS), (FAR, CROSS), ahead)

    def far_to_sib(r, h):
        return copy(0, h, r, 7, (FAR, SELF), (FAR, SIB), sibling)

    def await_piece(r, h, a, b):
        copy(0, h, r, 0, (a, b), (a, b), sibling).wait_recv()

    def send_own(r):
        own_to_across(r, 0).start()
        own_to_diagonal(r, 1).start()

        @pl.when(inner)
        def _():
            own_to_diagonal(r, 0).start()
            own_to_across(r, 1).start()

        own_to_sib(r, 0).start()
        own_to_sib(r, 1).start()

    def apply(r, a, b):
        dz = (1, dz_near, 2 - dz_near)[a]
        dy = (1, dy_sib, 2 - dy_sib)[b]
        base = dz * 9 + dy * 3
        for source in range(xb):
            targets = [x for x in (source - 1, source, source + 1) if 0 <= x < xb]
            rows = [oper[x, slot_ref[x, base + source - x + 1]] for x in targets]
            column = jnp.concatenate([halo[r, h, a, b, source] for h in range(HALVES)], axis=1)
            moved = jnp.dot(jnp.concatenate(rows, axis=0), column, preferred_element_type=F32)
            for i, x in enumerate(targets):
                residual[x] -= moved[i * width : (i + 1) * width]

    bound = bound_ref[0]
    sigma = 9.0 / 7.0
    theta = 9.0 * bound / 16.0
    delta = 7.0 * bound / 16.0
    rho_0 = 1.0 / sigma
    rho_1 = 1.0 / (2.0 * sigma - rho_0)
    rho_2 = 1.0 / (2.0 * sigma - rho_1)

    barrier = pltpu.get_barrier_semaphore()
    for device in (sibling, across, diagonal, opposite, ahead, behind):
        pl.semaphore_signal(barrier, inc=1, device_id=device, device_id_type=MESH)

    load_rhs.wait()

    def first_direction(x, carry):
        value = residual[x] / theta
        direction[x] = value
        smoothed[x] = value
        for h in range(HALVES):
            halo[0, h, OWN, SELF, x] = value[:, h * half : (h + 1) * half].astype(BF16)
        return carry

    lax.fori_loop(0, xb, first_direction, 0)
    pl.semaphore_wait(barrier, 6)
    send_own(0)
    load_diag.wait()
    for load in load_blocks:
        load.wait()
    load_restrict.wait()

    def one_round(r, carry):
        apply(r, OWN, SELF)
        await_piece(r, 0, OWN, CROSS)
        relay(r, 0).start()
        await_piece(r, 1, NEAR, CROSS)
        relay(r, 1).start()

        @pl.when(inner)
        def _():
            cross_to_ahead(r, 1).start()
            await_piece(r, 0, NEAR, CROSS)
            cross_to_ahead(r, 0).start()
            await_piece(r, 1, OWN, CROSS)

        for h in range(HALVES):
            await_piece(r, h, OWN, SIB)
        apply(r, OWN, SIB)
        for h in range(HALVES):
            await_piece(r, h, NEAR, SELF)
            near_to_ahead(r, h).start()
            near_to_sib(r, h).start()

        @pl.when(inner)
        def _():
            apply(r, OWN, CROSS)
            apply(r, NEAR, CROSS)

        apply(r, NEAR, SELF)
        for h in range(HALVES):
            await_piece(r, h, NEAR, SIB)
        apply(r, NEAR, SIB)

        for h in range(HALVES):
            await_piece(r, h, FAR, SELF)
            far_to_sib(r, h).start()

        @pl.when(inner)
        def _():
            for h in range(HALVES):
                await_piece(r, h, FAR, CROSS)

        @pl.when(inner & has_far)
        def _():
            apply(r, FAR, CROSS)

        @pl.when(has_far)
        def _():
            apply(r, FAR, SELF)

        for h in range(HALVES):
            await_piece(r, h, FAR, SIB)

        @pl.when(has_far)
        def _():
            apply(r, FAR, SIB)

        @pl.when(r < ROUNDS - 1)
        def _():
            scale = jnp.where(r == 0, rho_1 * rho_0, rho_2 * rho_1)
            gain = jnp.where(r == 0, 2.0 * rho_1 / delta, 2.0 * rho_2 / delta)

            def next_direction(x, carry):
                value = scale * direction[x] + gain * residual[x]
                direction[x] = value
                smoothed[x] += value
                for h in range(HALVES):
                    halo[r + 1, h, OWN, SELF, x] = value[:, h * half : (h + 1) * half].astype(BF16)
                return carry

            lax.fori_loop(0, xb, next_direction, 0)
            send_own(r + 1)

        return carry

    lax.fori_loop(0, ROUNDS, one_round, 0)

    store_smoothed = pltpu.make_async_copy(smoothed, smoothed_hbm, load_sem.at[0])
    store_smoothed.start()

    def restricted(pair):
        total = None
        for i in range(2):
            x = 2 * pair + i
            term = jnp.dot(restrict[kind_ref[x]], residual[x].astype(BF16), preferred_element_type=F32)
            total = term if total is None else total + term
        return total

    leaving[...] = restricted(1 - parity).astype(BF16)
    hand_over = pltpu.make_async_remote_copy(
        src_ref=leaving,
        dst_ref=arrived,
        send_sem=coarse_sem.at[0],
        recv_sem=coarse_sem.at[1],
        device_id=opposite,
        device_id_type=MESH,
    )
    hand_over.start()
    kept[...] = restricted(parity)

    def drain(r, carry):
        for h in range(HALVES):
            own_to_sib(r, h).wait_send()
            relay(r, h).wait_send()
            near_to_sib(r, h).wait_send()
            near_to_ahead(r, h).wait_send()
            far_to_sib(r, h).wait_send()
        own_to_across(r, 0).wait_send()
        own_to_diagonal(r, 1).wait_send()

        @pl.when(inner)
        def _():
            own_to_across(r, 1).wait_send()
            own_to_diagonal(r, 0).wait_send()
            for h in range(HALVES):
                cross_to_ahead(r, h).wait_send()

        return carry

    lax.fori_loop(0, ROUNDS, drain, 0)
    hand_over.wait()
    kept[...] += arrived[...].astype(F32)
    store_coarse = pltpu.make_async_copy(kept, coarse_hbm, load_sem.at[1])
    store_coarse.start()
    store_coarse.wait()
    store_smoothed.wait()


def on_device(layers, rhs, blocks, diag_blocks, neighbours, bound, restrict_blocks, restrict_kind):
    xb, width, cols = rhs.shape[2:]
    slots = blocks.shape[3]
    codes = neighbours[0, 0]
    codes = codes + (codes >= slots // 2).astype(jnp.int32)
    names = jnp.arange(slots + 1, dtype=jnp.int32)
    order = jnp.arange(slots, dtype=jnp.int32)
    slot_of = jnp.sum(jnp.where(codes[:, :, None] == names, order[:, None] - slots, 0), axis=1) + slots
    half = cols // HALVES
    smem = pl.BlockSpec(memory_space=pltpu.SMEM)
    hbm = pl.BlockSpec(memory_space=pl.ANY)
    smoothed, coarse = pl.pallas_call(
        functools.partial(smooth_kernel, layers),
        out_shape=(
            jax.ShapeDtypeStruct((xb, width, cols), F32),
            jax.ShapeDtypeStruct((width, cols), F32),
        ),
        in_specs=[smem, smem, smem, hbm, hbm, hbm, hbm],
        out_specs=(hbm, hbm),
        scratch_shapes=[
            pltpu.VMEM((xb, slots + 1, width, width), BF16),
            pltpu.VMEM((ROUNDS, HALVES, 3, 3, xb, width, half), BF16),
            pltpu.VMEM((xb, width, cols), F32),
            pltpu.VMEM((xb, width, cols), F32),
            pltpu.VMEM((xb, width, cols), F32),
            pltpu.VMEM(restrict_blocks.shape, BF16),
            pltpu.VMEM((width, cols), F32),
            pltpu.VMEM((width, cols), BF16),
            pltpu.VMEM((width, cols), BF16),
            pltpu.SemaphoreType.DMA((3 + xb,)),
            pltpu.SemaphoreType.DMA((ROUNDS, HALVES, 8)),
            pltpu.SemaphoreType.DMA((ROUNDS, HALVES, 9)),
            pltpu.SemaphoreType.DMA((2,)),
        ],
        compiler_params=pltpu.CompilerParams(
            collective_id=0, has_side_effects=True, vmem_limit_bytes=56 * 2**20
        ),
        cost_estimate=pl.CostEstimate(flops=6 * 10**9, bytes_accessed=11 * 10**6, transcendentals=0),
        name="smooth_and_restrict",
    )(slot_of, restrict_kind[0, 0], bound, rhs[0, 0], blocks[0, 0], diag_blocks[0, 0], restrict_blocks)
    return smoothed[None, None], coarse[None, None, None]


def solution(mesh):
    return jax.shard_map(
        functools.partial(on_device, mesh.shape["slab"]),
        mesh=mesh,
        in_specs=(
            P("slab", "quad", None, None, None),
            P("slab", "quad", None, None, None, None),
            P("slab", "quad", None, None, None),
            P("slab", "quad", None, None),
            P(),
            P(),
            P("slab", "quad", None),
        ),
        out_specs=(P("slab", "quad", None, None, None), P("slab", "quad", None, None, None)),
        check_vma=False,
    )
```

```python
import functools

import jax
import jax.numpy as jnp
from jax import lax
from jax.experimental import pallas as pl
from jax.experimental.pallas import tpu as pltpu
from jax.sharding import PartitionSpec as P

OWN, NEAR, FAR = 0, 1, 2
SELF, SIB, CROSS = 0, 1, 2
ROUNDS = 3
HALVES = 2
PIECES = 2
MESH = pl.DeviceIdType.MESH
F32 = jnp.float32
BF16 = jnp.bfloat16


def smooth_kernel(
    layers,
    slot_ref,
    kind_ref,
    bound_ref,
    rhs_hbm,
    blocks_hbm,
    diag_hbm,
    restrict_hbm,
    later_hbm,
    kept_hbm,
    arrived_hbm,
    oper,
    halo,
    residual,
    direction,
    later,
    restrict,
    kept,
    leaving,
    load_sem,
    store_sem,
    send_sem,
    recv_sem,
    coarse_sem,
):
    s = lax.axis_index("slab")
    q = lax.axis_index("quad")
    parity = lax.rem(s, 2)
    inner = (q == 1) | (q == 2)
    near_s = s + 1 - 2 * parity
    step = 2 - 4 * parity
    sibling = (s, q + 1 - 2 * lax.rem(q, 2))
    across = (s, 3 - q)
    diagonal = (near_s, 3 - q)
    opposite = (near_s, q)
    ahead = (lax.rem(s + step + layers, layers), q)
    behind = (lax.rem(s - step + layers, layers), q)
    dz_near = 2 - 2 * parity
    dy_sib = 2 - 2 * lax.rem(q, 2)
    has_far = jnp.where(parity == 0, s > 0, s < layers - 1)
    xb, width, half = residual.shape[1:]
    slots = blocks_hbm.shape[1]
    per_piece = xb // PIECES

    load_rhs = [
        pltpu.make_async_copy(rhs_hbm.at[:, :, pl.ds(h * half, half)], residual.at[h], load_sem.at[h])
        for h in range(HALVES)
    ]
    load_operator = [pltpu.make_async_copy(diag_hbm, oper.at[:, slots], load_sem.at[2])] + [
        pltpu.make_async_copy(blocks_hbm.at[x], oper.at[x, pl.ds(0, slots)], load_sem.at[3 + x]) for x in range(xb)
    ]
    load_restrict = pltpu.make_async_copy(restrict_hbm, restrict, load_sem.at[3 + xb])
    for load in load_rhs + load_operator + [load_restrict]:
        load.start()

    def copy(r, h, lane, src, dst, device, piece):
        blocks = pl.ds(piece * per_piece, per_piece)
        return pltpu.make_async_remote_copy(
            src_ref=halo.at[r, h, src[0], src[1], blocks],
            dst_ref=halo.at[r, h, dst[0], dst[1], blocks],
            send_sem=send_sem.at[r, h, lane, piece],
            recv_sem=recv_sem.at[r, h, dst[0] * 3 + dst[1], piece],
            device_id=device,
            device_id_type=MESH,
        )

    def own_to_sib(r, h, piece):
        return copy(r, h, 0, (OWN, SELF), (OWN, SIB), sibling, piece)

    def own_to_across(r, h, piece):
        return copy(r, h, 1, (OWN, SELF), (OWN, CROSS), across, piece)

    def own_to_diagonal(r, h, piece):
        return copy(r, h, 2, (OWN, SELF), (NEAR, CROSS), diagonal, piece)

    def own_to_opposite(r, h, piece):
        return copy(r, h, 3, (OWN, SELF), (NEAR, SELF), opposite, piece)

    def near_to_sib(r, h, piece):
        return copy(r, h, 4, (NEAR, SELF), (NEAR, SIB), sibling, piece)

    def near_to_ahead(r, h, piece):
        return copy(r, h, 5, (NEAR, SELF), (FAR, SELF), ahead, piece)

    def cross_to_ahead(r, h, piece):
        return copy(r, h, 6, (NEAR, CROSS), (FAR, CROSS), ahead, piece)

    def far_to_sib(r, h, piece):
        return copy(r, h, 7, (FAR, SELF), (FAR, SIB), sibling, piece)

    def await_piece(r, h, a, b, piece):
        copy(r, h, 0, (a, b), (a, b), sibling, piece).wait_recv()

    def await_row(r, h, a, b):
        for piece in range(PIECES):
            await_piece(r, h, a, b, piece)

    def send_own(r, h):
        for piece in range(PIECES):
            own_to_opposite(r, h, piece).start()

        @pl.when(inner)
        def _():
            for piece in range(PIECES):
                own_to_diagonal(r, h, piece).start()

        for piece in range(PIECES):
            own_to_sib(r, h, piece).start()

        @pl.when(inner)
        def _():
            for piece in range(PIECES):
                own_to_across(r, h, piece).start()

    def apply(r, h, a, b):
        dz = (1, dz_near, 2 - dz_near)[a]
        dy = (1, dy_sib, 2 - dy_sib)[b]
        base = dz * 9 + dy * 3
        for source in range(xb):
            targets = [x for x in (source - 1, source, source + 1) if 0 <= x < xb]
            rows = [oper[x, slot_ref[x, base + source - x + 1]] for x in targets]
            moved = jnp.dot(jnp.concatenate(rows, axis=0), halo[r, h, a, b, source], preferred_element_type=F32)
            for i, x in enumerate(targets):
                residual[h, x] -= moved[i * width : (i + 1) * width]

    bound = bound_ref[0]
    sigma = 9.0 / 7.0
    theta = 9.0 * bound / 16.0
    delta = 7.0 * bound / 16.0
    rho_0 = 1.0 / sigma
    rho_1 = 1.0 / (2.0 * sigma - rho_0)
    rho_2 = 1.0 / (2.0 * sigma - rho_1)

    def hand_over(h):
        return pltpu.make_async_remote_copy(
            src_ref=leaving.at[h],
            dst_ref=arrived_hbm.at[h],
            send_sem=coarse_sem.at[0, h],
            recv_sem=coarse_sem.at[1, h],
            device_id=opposite,
            device_id_type=MESH,
        )

    def store_later(h):
        return pltpu.make_async_copy(
            later.at[h], later_hbm.at[:, :, pl.ds(pl.multiple_of(h * half, half), half)], store_sem.at[0, h]
        )

    def store_kept(h):
        return pltpu.make_async_copy(
            kept.at[h], kept_hbm.at[:, pl.ds(pl.multiple_of(h * half, half), half)], store_sem.at[1, h]
        )

    def restricted(h, pair):
        total = None
        for i in range(2):
            x = 2 * pair + i
            term = jnp.dot(restrict[kind_ref[x]], residual[h, x].astype(BF16), preferred_element_type=F32)
            total = term if total is None else total + term
        return total

    def finish(r, h):
        @pl.when(r < ROUNDS - 1)
        def _():
            first = r == 0
            scale = jnp.where(first, rho_1 * rho_0, rho_2 * rho_1)
            gain = jnp.where(first, 2.0 * rho_1 / delta, 2.0 * rho_2 / delta)
            keep = jnp.where(first, 0.0, 1.0)

            def next_direction(x, carry):
                before = direction[h, x]
                value = scale * before + gain * residual[h, x]
                direction[h, x] = value
                later[h, x] = value + keep * before
                halo[r + 1, h, OWN, SELF, x] = value.astype(BF16)
                return carry

            lax.fori_loop(0, xb, next_direction, 0)
            send_own(r + 1, h)

        @pl.when(r == ROUNDS - 2)
        def _():
            store_later(h).start()

        @pl.when(r == ROUNDS - 1)
        def _():
            leaving[h] = restricted(h, 1 - parity).astype(BF16)
            hand_over(h).start()
            kept[h] = restricted(h, parity)
            store_kept(h).start()

    def half_step(t, older=True, newer=True):
        if older:
            r, h = lax.div(t - 1, HALVES), lax.rem(t - 1, HALVES)
        if newer:
            rn, hn = lax.div(t, HALVES), lax.rem(t, HALVES)

        def pass_near(piece):
            await_piece(rn, hn, NEAR, SELF, piece)
            near_to_ahead(rn, hn, piece).start()
            near_to_sib(rn, hn, piece).start()

        def pass_far(piece):
            await_piece(r, h, FAR, SELF, piece)
            far_to_sib(r, h, piece).start()

        if older:

            @pl.when(inner)
            def _():
                for piece in range(PIECES):
                    await_piece(r, h, NEAR, CROSS, piece)
                    cross_to_ahead(r, h, piece).start()

            await_row(r, h, OWN, SIB)
            apply(r, h, OWN, SIB)
            apply(r, h, NEAR, SELF)
            pass_far(0)
            await_row(r, h, NEAR, SIB)
            apply(r, h, NEAR, SIB)

            @pl.when(inner)
            def _():
                await_row(r, h, OWN, CROSS)
                apply(r, h, OWN, CROSS)
                apply(r, h, NEAR, CROSS)

            pass_far(1)
        if newer:
            pass_near(0)
        if older:

            @pl.when(has_far)
            def _():
                apply(r, h, FAR, SELF)

        if newer:
            pass_near(1)
        if older:
            await_row(r, h, FAR, SIB)

            @pl.when(has_far)
            def _():
                apply(r, h, FAR, SIB)

            @pl.when(inner)
            def _():
                await_row(r, h, FAR, CROSS)

            @pl.when(inner & has_far)
            def _():
                apply(r, h, FAR, CROSS)

            finish(r, h)
        if newer:
            apply(rn, hn, OWN, SELF)

    barrier = pltpu.get_barrier_semaphore()
    for device in (sibling, across, diagonal, opposite, ahead, behind):
        pl.semaphore_signal(barrier, inc=1, device_id=device, device_id_type=MESH)

    for h in range(HALVES):
        load_rhs[h].wait()

        def first_direction(x, carry):
            value = residual[h, x] / theta
            direction[h, x] = value
            halo[0, h, OWN, SELF, x] = value.astype(BF16)
            return carry

        lax.fori_loop(0, xb, first_direction, 0)
        if h == 0:
            pl.semaphore_wait(barrier, 6)
        send_own(0, h)
    for load in load_operator + [load_restrict]:
        load.wait()

    steps = ROUNDS * HALVES
    half_step(0, older=False)

    def middle(t, carry):
        half_step(t)
        return carry

    lax.fori_loop(1, steps, middle, 0)
    half_step(steps, newer=False)

    def drain(r, carry):
        for h in range(HALVES):
            for piece in range(PIECES):
                own_to_sib(r, h, piece).wait_send()
                own_to_opposite(r, h, piece).wait_send()
                near_to_sib(r, h, piece).wait_send()
                near_to_ahead(r, h, piece).wait_send()
                far_to_sib(r, h, piece).wait_send()

        @pl.when(inner)
        def _():
            for h in range(HALVES):
                for piece in range(PIECES):
                    own_to_across(r, h, piece).wait_send()
                    own_to_diagonal(r, h, piece).wait_send()
                    cross_to_ahead(r, h, piece).wait_send()

        return carry

    lax.fori_loop(0, ROUNDS, drain, 0)
    for h in range(HALVES):
        store_later(h).wait()
        store_kept(h).wait()
        hand_over(h).wait()


def on_device(layers, rhs, blocks, diag_blocks, neighbours, bound, restrict_blocks, restrict_kind):
    xb, width, cols = rhs.shape[2:]
    slots = blocks.shape[3]
    codes = neighbours[0, 0]
    codes = codes + (codes >= slots // 2).astype(jnp.int32)
    names = jnp.arange(slots + 1, dtype=jnp.int32)
    order = jnp.arange(slots, dtype=jnp.int32)
    slot_of = jnp.sum(jnp.where(codes[:, :, None] == names, order[:, None] - slots, 0), axis=1) + slots
    half = cols // HALVES
    smem = pl.BlockSpec(memory_space=pltpu.SMEM)
    hbm = pl.BlockSpec(memory_space=pl.ANY)
    later, kept, arrived = pl.pallas_call(
        functools.partial(smooth_kernel, layers),
        out_shape=(
            jax.ShapeDtypeStruct((xb, width, cols), F32),
            jax.ShapeDtypeStruct((width, cols), F32),
            jax.ShapeDtypeStruct((HALVES, width, half), BF16),
        ),
        in_specs=[smem, smem, smem, hbm, hbm, hbm, hbm],
        out_specs=(hbm, hbm, hbm),
        scratch_shapes=[
            pltpu.VMEM((xb, slots + 1, width, width), BF16),
            pltpu.VMEM((ROUNDS, HALVES, 3, 3, xb, width, half), BF16),
            pltpu.VMEM((HALVES, xb, width, half), F32),
            pltpu.VMEM((HALVES, xb, width, half), F32),
            pltpu.VMEM((HALVES, xb, width, half), F32),
            pltpu.VMEM(restrict_blocks.shape, BF16),
            pltpu.VMEM((HALVES, width, half), F32),
            pltpu.VMEM((HALVES, width, half), BF16),
            pltpu.SemaphoreType.DMA((4 + xb,)),
            pltpu.SemaphoreType.DMA((2, HALVES)),
            pltpu.SemaphoreType.DMA((ROUNDS, HALVES, 8, PIECES)),
            pltpu.SemaphoreType.DMA((ROUNDS, HALVES, 9, PIECES)),
            pltpu.SemaphoreType.DMA((2, HALVES)),
        ],
        compiler_params=pltpu.CompilerParams(
            collective_id=0, has_side_effects=True, vmem_limit_bytes=56 * 2**20
        ),
        cost_estimate=pl.CostEstimate(flops=6 * 10**9, bytes_accessed=11 * 10**6, transcendentals=0),
        name="smooth_and_restrict",
    )(slot_of, restrict_kind[0, 0], bound, rhs[0, 0], blocks[0, 0], diag_blocks[0, 0], restrict_blocks)
    smoothed = later + rhs[0, 0] / (9.0 * bound[0] / 16.0)
    coarse = kept + jnp.concatenate([arrived[h] for h in range(HALVES)], axis=1).astype(F32)
    return smoothed[None, None], coarse[None, None, None]


def solution(mesh):
    return jax.shard_map(
        functools.partial(on_device, mesh.shape["slab"]),
        mesh=mesh,
        in_specs=(
            P("slab", "quad", None, None, None),
            P("slab", "quad", None, None, None, None),
            P("slab", "quad", None, None, None),
            P("slab", "quad", None, None),
            P(),
            P(),
            P("slab", "quad", None),
        ),
        out_specs=(P("slab", "quad", None, None, None), P("slab", "quad", None, None, None)),
        check_vma=False,
    )
```

```python
import functools

import jax
import jax.numpy as jnp
from jax import lax
from jax.experimental import pallas as pl
from jax.experimental.pallas import tpu as pltpu
from jax.sharding import PartitionSpec as P

OWN, NEAR, FAR = 0, 1, 2
SELF, SIB, CROSS = 0, 1, 2
ROUNDS = 3
HALVES = 2
PAIRS = (0, 2)
MESH = pl.DeviceIdType.MESH
F32 = jnp.float32
BF16 = jnp.bfloat16


def smooth_kernel(
    layers,
    kind_ref,
    bound_ref,
    code_hbm,
    rhs_hbm,
    blocks_hbm,
    diag_hbm,
    restrict_hbm,
    smoothed_hbm,
    kept_hbm,
    arrived_hbm,
    oper,
    halo,
    residual,
    direction,
    smoothed,
    restrict,
    kept,
    leaving,
    codes,
    columns,
    slot_ref,
    load_sem,
    store_sem,
    send_sem,
    recv_sem,
    coarse_sem,
):
    s = lax.axis_index("slab")
    q = lax.axis_index("quad")
    parity = lax.rem(s, 2)
    inner = (q == 1) | (q == 2)
    near_s = s + 1 - 2 * parity
    step = 2 - 4 * parity
    sibling = (s, q + 1 - 2 * lax.rem(q, 2))
    across = (s, 3 - q)
    diagonal = (near_s, 3 - q)
    opposite = (near_s, q)
    ahead = (lax.rem(s + step + layers, layers), q)
    behind = (lax.rem(s - step + layers, layers), q)
    dz_near = 2 - 2 * parity
    dy_sib = 2 - 2 * lax.rem(q, 2)
    has_far = jnp.where(parity == 0, s > 0, s < layers - 1)
    xb, width, half = residual.shape[1:]
    slots = blocks_hbm.shape[1]

    load_rhs = [
        pltpu.make_async_copy(rhs_hbm.at[:, :, pl.ds(h * half, half)], residual.at[h], load_sem.at[h])
        for h in range(HALVES)
    ]
    load_operator = [pltpu.make_async_copy(diag_hbm, oper.at[:, slots], load_sem.at[2])] + [
        pltpu.make_async_copy(blocks_hbm.at[x], oper.at[x, pl.ds(0, slots)], load_sem.at[3 + x]) for x in range(xb)
    ]
    load_restrict = pltpu.make_async_copy(restrict_hbm, restrict, load_sem.at[3 + xb])
    load_codes = pltpu.make_async_copy(code_hbm, codes, load_sem.at[4 + xb])
    place_slots = pltpu.make_async_copy(columns, slot_ref, load_sem.at[5 + xb])
    load_codes.start()
    for load in load_rhs + load_operator + [load_restrict]:
        load.start()

    def copy(r, h, lane, src, dst, device, first, count):
        blocks = pl.ds(first, count)
        return pltpu.make_async_remote_copy(
            src_ref=halo.at[r, h, src[0], src[1], blocks],
            dst_ref=halo.at[r, h, dst[0], dst[1], blocks],
            send_sem=send_sem.at[r, h, lane, first],
            recv_sem=recv_sem.at[r, h, dst[0] * 3 + dst[1], first],
            device_id=device,
            device_id_type=MESH,
        )

    def own_to_sib(r, h, first):
        return copy(r, h, 0, (OWN, SELF), (OWN, SIB), sibling, first, 2)

    def own_to_across(r, h, first):
        return copy(r, h, 1, (OWN, SELF), (OWN, CROSS), across, first, 2)

    def own_to_diagonal(r, h, first):
        return copy(r, h, 2, (OWN, SELF), (NEAR, CROSS), diagonal, first, 2)

    def own_to_opposite(r, h, first):
        return copy(r, h, 3, (OWN, SELF), (NEAR, SELF), opposite, first, 1)

    def near_to_sib(r, h, first):
        return copy(r, h, 4, (NEAR, SELF), (NEAR, SIB), sibling, first, 2)

    def near_to_ahead(r, h, first):
        return copy(r, h, 5, (NEAR, SELF), (FAR, SELF), ahead, first, 1)

    def cross_to_ahead(r, h, first):
        return copy(r, h, 6, (NEAR, CROSS), (FAR, CROSS), ahead, first, 2)

    def far_to_sib(r, h, first):
        return copy(r, h, 7, (FAR, SELF), (FAR, SIB), sibling, first, 1)

    def await_piece(r, h, a, b, first, count):
        copy(r, h, 0, (a, b), (a, b), sibling, first, count).wait_recv()

    def await_pairs(r, h, a, b):
        for first in PAIRS:
            await_piece(r, h, a, b, first, 2)

    def send_pair(r, h, first):
        @pl.when(inner)
        def _():
            own_to_diagonal(r, h, first).start()

        own_to_sib(r, h, first).start()

        @pl.when(inner)
        def _():
            own_to_across(r, h, first).start()

    def apply(r, h, a, b, sources=range(4)):
        dz = (1, dz_near, 2 - dz_near)[a]
        dy = (1, dy_sib, 2 - dy_sib)[b]
        base = dz * 9 + dy * 3
        for source in sources:
            targets = [x for x in (source - 1, source, source + 1) if 0 <= x < xb]
            rows = [oper[x, slot_ref[base + source - x + 1, x]] for x in targets]
            moved = jnp.dot(jnp.concatenate(rows, axis=0), halo[r, h, a, b, source], preferred_element_type=F32)
            for i, x in enumerate(targets):
                residual[h, x] -= moved[i * width : (i + 1) * width]

    bound = bound_ref[0]
    sigma = 9.0 / 7.0
    theta = 9.0 * bound / 16.0
    delta = 7.0 * bound / 16.0
    rho_0 = 1.0 / sigma
    rho_1 = 1.0 / (2.0 * sigma - rho_0)
    rho_2 = 1.0 / (2.0 * sigma - rho_1)

    def hand_over(h):
        return pltpu.make_async_remote_copy(
            src_ref=leaving.at[h],
            dst_ref=arrived_hbm.at[h],
            send_sem=coarse_sem.at[0, h],
            recv_sem=coarse_sem.at[1, h],
            device_id=opposite,
            device_id_type=MESH,
        )

    def store_smoothed(h):
        return pltpu.make_async_copy(
            smoothed.at[h], smoothed_hbm.at[:, :, pl.ds(pl.multiple_of(h * half, half), half)], store_sem.at[0, h]
        )

    def store_kept(h):
        return pltpu.make_async_copy(
            kept.at[h], kept_hbm.at[:, pl.ds(pl.multiple_of(h * half, half), half)], store_sem.at[1, h]
        )

    def restricted(h, pair):
        total = None
        for i in range(2):
            x = 2 * pair + i
            term = jnp.dot(restrict[kind_ref[x]], residual[h, x].astype(BF16), preferred_element_type=F32)
            total = term if total is None else total + term
        return total

    def advance(r, h, targets):
        @pl.when(r < ROUNDS - 1)
        def _():
            first = r == 0
            scale = jnp.where(first, rho_1 * rho_0, rho_2 * rho_1)
            gain = jnp.where(first, 2.0 * rho_1 / delta, 2.0 * rho_2 / delta)
            for x in targets:
                value = scale * direction[h, x] + gain * residual[h, x]
                direction[h, x] = value
                smoothed[h, x] += value
                halo[r + 1, h, OWN, SELF, x] = value.astype(BF16)
                own_to_opposite(r + 1, h, x).start()
                if x % 2 == 1:
                    send_pair(r + 1, h, x - 1)

    def finish(r, h):
        @pl.when(r == ROUNDS - 2)
        def _():
            store_smoothed(h).start()

        @pl.when(r == ROUNDS - 1)
        def _():
            leaving[h] = restricted(h, 1 - parity).astype(BF16)
            hand_over(h).start()
            kept[h] = restricted(h, parity)
            store_kept(h).start()

    def half_step(t, last=True, older=True, newer=True):
        if last:
            rl, hl = lax.div(t - 2, HALVES), lax.rem(t, HALVES)
        if older:
            r, h = lax.div(t - 1, HALVES), lax.rem(t - 1, HALVES)
        if newer:
            rn, hn = lax.div(t, HALVES), lax.rem(t, HALVES)

        def pass_near(r, h, x):
            await_piece(r, h, NEAR, SELF, x, 1)
            near_to_ahead(r, h, x).start()
            if x % 2 == 1:
                near_to_sib(r, h, x - 1).start()

        def pass_far(x):
            await_piece(r, h, FAR, SELF, x, 1)
            far_to_sib(r, h, x).start()

        def far_blocks(row, sources):
            @pl.when((inner & has_far) if row == CROSS else has_far)
            def _():
                apply(r, h, FAR, row, sources)

        if older:
            pass_near(r, h, 3)

            @pl.when(inner)
            def _():
                for first in PAIRS:
                    await_piece(r, h, NEAR, CROSS, first, 2)
                    cross_to_ahead(r, h, first).start()

            apply(r, h, OWN, SELF)
        if last:
            await_piece(rl, hl, FAR, SIB, 3, 1)

            @pl.when(has_far)
            def _():
                apply(rl, hl, FAR, SIB, (3,))

            advance(rl, hl, (2, 3))
            finish(rl, hl)
        if older:
            await_pairs(r, h, OWN, SIB)
            apply(r, h, OWN, SIB)
            pass_far(0)
            apply(r, h, NEAR, SELF)

            @pl.when(inner)
            def _():
                await_pairs(r, h, OWN, CROSS)
                apply(r, h, OWN, CROSS)

            pass_far(1)
        if newer:
            pass_near(rn, hn, 0)
        if older:
            await_pairs(r, h, NEAR, SIB)
            apply(r, h, NEAR, SIB)

            @pl.when(inner)
            def _():
                apply(r, h, NEAR, CROSS)

            far_blocks(SELF, (0, 1))
            pass_far(2)
            for x in (0, 1):
                await_piece(r, h, FAR, SIB, x, 1)
            far_blocks(SIB, (0, 1))

            @pl.when(inner)
            def _():
                await_piece(r, h, FAR, CROSS, 0, 2)

            far_blocks(CROSS, (0, 1))
            advance(r, h, (0,))
        if newer:
            pass_near(rn, hn, 1)
            pass_near(rn, hn, 2)
        if older:
            pass_far(3)
            far_blocks(SELF, (2, 3))

            @pl.when(inner)
            def _():
                await_piece(r, h, FAR, CROSS, 2, 2)

            far_blocks(CROSS, (2, 3))
            await_piece(r, h, FAR, SIB, 2, 1)
            far_blocks(SIB, (2,))
            advance(r, h, (1,))

    barrier = pltpu.get_barrier_semaphore()
    for device in (sibling, across, diagonal, opposite, ahead, behind):
        pl.semaphore_signal(barrier, inc=1, device_id=device, device_id_type=MESH)

    for h in range(HALVES):
        load_rhs[h].wait()

        def first_direction(x, carry):
            value = residual[h, x] / theta
            direction[h, x] = value
            smoothed[h, x] = value
            halo[0, h, OWN, SELF, x] = value.astype(BF16)
            return carry

        lax.fori_loop(0, xb, first_direction, 0)
        if h == 0:
            pl.semaphore_wait(barrier, 6)
        for x in range(xb):
            own_to_opposite(0, h, x).start()
        for first in PAIRS:
            send_pair(0, h, first)

    load_codes.wait()
    shape = (columns.shape[0], slots)
    offset = lax.broadcasted_iota(jnp.int32, shape, 0)
    slot = lax.broadcasted_iota(jnp.int32, shape, 1)
    lane = lax.broadcasted_iota(jnp.int32, columns.shape, 1)
    table = jnp.zeros(columns.shape, jnp.int32)
    for x in range(xb):
        named = codes[pl.ds(x, 1), :]
        named = named + jnp.where(named >= slots // 2, 1, 0)
        found = jnp.min(jnp.where(named == offset, slot, slots), axis=1, keepdims=True)
        table = jnp.where(lane == x, found, table)
    columns[...] = table
    place_slots.start()
    for load in load_operator + [load_restrict, place_slots]:
        load.wait()

    steps = ROUNDS * HALVES
    half_step(0, last=False, older=False)
    half_step(1, last=False)

    def middle(t, carry):
        half_step(t)
        return carry

    lax.fori_loop(2, steps, middle, 0)
    half_step(steps, newer=False)
    half_step(steps + 1, older=False, newer=False)

    def drain(r, carry):
        for h in range(HALVES):
            for x in range(xb):
                own_to_opposite(r, h, x).wait_send()
                near_to_ahead(r, h, x).wait_send()
                far_to_sib(r, h, x).wait_send()
            for first in PAIRS:
                own_to_sib(r, h, first).wait_send()
                near_to_sib(r, h, first).wait_send()

        @pl.when(inner)
        def _():
            for h in range(HALVES):
                for first in PAIRS:
                    own_to_across(r, h, first).wait_send()
                    own_to_diagonal(r, h, first).wait_send()
                    cross_to_ahead(r, h, first).wait_send()

        return carry

    lax.fori_loop(0, ROUNDS, drain, 0)
    for h in range(HALVES):
        store_smoothed(h).wait()
        store_kept(h).wait()
        hand_over(h).wait()


def outputs_kernel(smoothed_in, kept_in, arrived_in, smoothed_out, coarse_out, smoothed, coarse, arrived, sem):
    load_arrived = pltpu.make_async_copy(arrived_in, arrived, sem.at[0])
    load_kept = pltpu.make_async_copy(kept_in, coarse, sem.at[1])
    store = pltpu.make_async_copy(coarse, coarse_out, sem.at[2])
    load_arrived.start()
    load_kept.start()
    blocks = range(smoothed.shape[0])
    loads = [pltpu.make_async_copy(smoothed_in.at[x], smoothed.at[x], sem.at[3 + 2 * x]) for x in blocks]
    stores = [pltpu.make_async_copy(smoothed.at[x], smoothed_out.at[x], sem.at[4 + 2 * x]) for x in blocks]
    for load in loads:
        load.start()
    load_arrived.wait()
    load_kept.wait()
    coarse[...] += jnp.concatenate([arrived[h] for h in range(HALVES)], axis=1).astype(F32)
    store.start()
    for x in blocks:
        loads[x].wait()
        stores[x].start()
    for x in blocks:
        stores[x].wait()
    store.wait()


def on_device(layers, rhs, blocks, diag_blocks, neighbours, bound, restrict_blocks, restrict_kind):
    xb, width, cols = rhs.shape[2:]
    slots = blocks.shape[3]
    half = cols // HALVES
    smem = pl.BlockSpec(memory_space=pltpu.SMEM)
    hbm = pl.BlockSpec(memory_space=pl.ANY)
    smoothed, kept, arrived = pl.pallas_call(
        functools.partial(smooth_kernel, layers),
        out_shape=(
            jax.ShapeDtypeStruct((xb, width, cols), F32),
            jax.ShapeDtypeStruct((width, cols), F32),
            jax.ShapeDtypeStruct((HALVES, width, half), BF16),
        ),
        in_specs=[smem, smem, hbm, hbm, hbm, hbm, hbm],
        out_specs=(hbm, hbm, hbm),
        scratch_shapes=[
            pltpu.VMEM((xb, slots + 1, width, width), BF16),
            pltpu.VMEM((ROUNDS, HALVES, 3, 3, xb, width, half), BF16),
            pltpu.VMEM((HALVES, xb, width, half), F32),
            pltpu.VMEM((HALVES, xb, width, half), F32),
            pltpu.VMEM((HALVES, xb, width, half), F32),
            pltpu.VMEM(restrict_blocks.shape, BF16),
            pltpu.VMEM((HALVES, width, half), F32),
            pltpu.VMEM((HALVES, width, half), BF16),
            pltpu.VMEM((xb, slots), jnp.int32),
            pltpu.VMEM((32, 128), jnp.int32),
            pltpu.SMEM((32, 128), jnp.int32),
            pltpu.SemaphoreType.DMA((6 + xb,)),
            pltpu.SemaphoreType.DMA((2, HALVES)),
            pltpu.SemaphoreType.DMA((ROUNDS, HALVES, 8, xb)),
            pltpu.SemaphoreType.DMA((ROUNDS, HALVES, 9, xb)),
            pltpu.SemaphoreType.DMA((2, HALVES)),
        ],
        compiler_params=pltpu.CompilerParams(
            collective_id=0, has_side_effects=True, vmem_limit_bytes=56 * 2**20
        ),
        cost_estimate=pl.CostEstimate(flops=6 * 10**9, bytes_accessed=11 * 10**6, transcendentals=0),
        name="smooth_and_restrict",
    )(restrict_kind[0, 0], bound, neighbours[0, 0], rhs[0, 0], blocks[0, 0], diag_blocks[0, 0], restrict_blocks)
    smoothed, coarse = pl.pallas_call(
        outputs_kernel,
        out_shape=(
            jax.ShapeDtypeStruct((xb, width, cols), F32),
            jax.ShapeDtypeStruct((width, cols), F32),
        ),
        in_specs=[hbm, hbm, hbm],
        out_specs=(hbm, hbm),
        scratch_shapes=[
            pltpu.VMEM((xb, width, cols), F32),
            pltpu.VMEM((width, cols), F32),
            pltpu.VMEM((HALVES, width, half), BF16),
            pltpu.SemaphoreType.DMA((3 + 2 * xb,)),
        ],
        compiler_params=pltpu.CompilerParams(vmem_limit_bytes=56 * 2**20),
        name="outputs",
    )(smoothed, kept, arrived)
    return smoothed[None, None], coarse[None, None, None]


def solution(mesh):
    return jax.shard_map(
        functools.partial(on_device, mesh.shape["slab"]),
        mesh=mesh,
        in_specs=(
            P("slab", "quad", None, None, None),
            P("slab", "quad", None, None, None, None),
            P("slab", "quad", None, None, None),
            P("slab", "quad", None, None),
            P(),
            P(),
            P("slab", "quad", None),
        ),
        out_specs=(P("slab", "quad", None, None, None), P("slab", "quad", None, None, None)),
        check_vma=False,
    )
```

```python
import functools

import jax
import jax.numpy as jnp
from jax import lax
from jax.experimental import pallas as pl
from jax.experimental.pallas import tpu as pltpu
from jax.sharding import PartitionSpec as P

OWN, NEAR, FAR = 0, 1, 2
SELF, SIB, CROSS = 0, 1, 2
ROUNDS = 3
HALVES = 2
PAIRS = (0, 2)
MESH = pl.DeviceIdType.MESH
F32 = jnp.float32
BF16 = jnp.bfloat16


def smooth_kernel(
    layers,
    kind_ref,
    bound_ref,
    code_hbm,
    rhs_hbm,
    blocks_hbm,
    diag_hbm,
    restrict_hbm,
    smoothed_hbm,
    kept_hbm,
    arrived_hbm,
    oper,
    halo,
    residual,
    direction,
    smoothed,
    restrict,
    kept,
    leaving,
    codes,
    columns,
    slot_ref,
    load_sem,
    store_sem,
    send_sem,
    recv_sem,
    coarse_sem,
):
    s = lax.axis_index("slab")
    q = lax.axis_index("quad")
    parity = lax.rem(s, 2)
    inner = (q == 1) | (q == 2)
    near_s = s + 1 - 2 * parity
    step = 2 - 4 * parity
    sibling = (s, q + 1 - 2 * lax.rem(q, 2))
    across = (s, 3 - q)
    diagonal = (near_s, 3 - q)
    opposite = (near_s, q)
    ahead = (lax.rem(s + step + layers, layers), q)
    behind = (lax.rem(s - step + layers, layers), q)
    dz_near = 2 - 2 * parity
    dy_sib = 2 - 2 * lax.rem(q, 2)
    has_far = jnp.where(parity == 0, s > 0, s < layers - 1)
    xb, width, half = residual.shape[1:]
    slots = blocks_hbm.shape[1]

    load_rhs = [
        pltpu.make_async_copy(rhs_hbm.at[:, :, pl.ds(h * half, half)], residual.at[h], load_sem.at[h])
        for h in range(HALVES)
    ]
    load_operator = [pltpu.make_async_copy(diag_hbm, oper.at[:, slots], load_sem.at[2])] + [
        pltpu.make_async_copy(blocks_hbm.at[x], oper.at[x, pl.ds(0, slots)], load_sem.at[3 + x]) for x in range(xb)
    ]
    load_restrict = pltpu.make_async_copy(restrict_hbm, restrict, load_sem.at[3 + xb])
    load_codes = pltpu.make_async_copy(code_hbm, codes, load_sem.at[4 + xb])
    place_slots = pltpu.make_async_copy(columns, slot_ref, load_sem.at[5 + xb])
    load_codes.start()
    for load in load_rhs:
        load.start()

    def copy(r, h, lane, src, dst, device, first, count):
        blocks = pl.ds(first, count)
        return pltpu.make_async_remote_copy(
            src_ref=halo.at[r, h, src[0], src[1], blocks],
            dst_ref=halo.at[r, h, dst[0], dst[1], blocks],
            send_sem=send_sem.at[r, h, lane, first],
            recv_sem=recv_sem.at[r, h, dst[0] * 3 + dst[1], first],
            device_id=device,
            device_id_type=MESH,
        )

    def own_to_sib(r, h, first):
        return copy(r, h, 0, (OWN, SELF), (OWN, SIB), sibling, first, 2)

    def own_to_across(r, h, first):
        return copy(r, h, 1, (OWN, SELF), (OWN, CROSS), across, first, 2)

    def own_to_diagonal(r, h, first):
        return copy(r, h, 2, (OWN, SELF), (NEAR, CROSS), diagonal, first, 2)

    def own_to_opposite(r, h, first):
        return copy(r, h, 3, (OWN, SELF), (NEAR, SELF), opposite, first, 1)

    def near_to_sib(r, h, first):
        return copy(r, h, 4, (NEAR, SELF), (NEAR, SIB), sibling, first, 2)

    def near_to_ahead(r, h, first):
        return copy(r, h, 5, (NEAR, SELF), (FAR, SELF), ahead, first, 1)

    def cross_to_ahead(r, h, first):
        return copy(r, h, 6, (NEAR, CROSS), (FAR, CROSS), ahead, first, 2)

    def far_to_sib(r, h, first):
        return copy(r, h, 7, (FAR, SELF), (FAR, SIB), sibling, first, 1)

    def await_piece(r, h, a, b, first, count):
        copy(r, h, 0, (a, b), (a, b), sibling, first, count).wait_recv()

    def await_pairs(r, h, a, b):
        for first in PAIRS:
            await_piece(r, h, a, b, first, 2)

    def send_pair(r, h, first):
        @pl.when(inner)
        def _():
            own_to_diagonal(r, h, first).start()

        own_to_sib(r, h, first).start()

        @pl.when(inner)
        def _():
            own_to_across(r, h, first).start()

    def apply(r, h, a, b, sources=range(4)):
        dz = (1, dz_near, 2 - dz_near)[a]
        dy = (1, dy_sib, 2 - dy_sib)[b]
        base = dz * 9 + dy * 3
        for source in sources:
            targets = [x for x in (source - 1, source, source + 1) if 0 <= x < xb]
            rows = [oper[x, slot_ref[base + source - x + 1, x]] for x in targets]
            moved = jnp.dot(jnp.concatenate(rows, axis=0), halo[r, h, a, b, source], preferred_element_type=F32)
            for i, x in enumerate(targets):
                residual[h, x] -= moved[i * width : (i + 1) * width]

    bound = bound_ref[0]
    sigma = 9.0 / 7.0
    theta = 9.0 * bound / 16.0
    delta = 7.0 * bound / 16.0
    rho_0 = 1.0 / sigma
    rho_1 = 1.0 / (2.0 * sigma - rho_0)
    rho_2 = 1.0 / (2.0 * sigma - rho_1)

    def hand_over(h):
        return pltpu.make_async_remote_copy(
            src_ref=leaving.at[h],
            dst_ref=arrived_hbm.at[h],
            send_sem=coarse_sem.at[0, h],
            recv_sem=coarse_sem.at[1, h],
            device_id=opposite,
            device_id_type=MESH,
        )

    def store_smoothed(h):
        return pltpu.make_async_copy(
            smoothed.at[h], smoothed_hbm.at[:, :, pl.ds(pl.multiple_of(h * half, half), half)], store_sem.at[0, h]
        )

    def store_kept(h):
        return pltpu.make_async_copy(
            kept.at[h], kept_hbm.at[:, pl.ds(pl.multiple_of(h * half, half), half)], store_sem.at[1, h]
        )

    def restricted(h, pair):
        total = None
        for i in range(2):
            x = 2 * pair + i
            term = jnp.dot(restrict[kind_ref[x]], residual[h, x].astype(BF16), preferred_element_type=F32)
            total = term if total is None else total + term
        return total

    def advance(r, h, targets):
        @pl.when(r < ROUNDS - 1)
        def _():
            first = r == 0
            scale = jnp.where(first, rho_1 * rho_0, rho_2 * rho_1)
            gain = jnp.where(first, 2.0 * rho_1 / delta, 2.0 * rho_2 / delta)
            for x in targets:
                value = scale * direction[h, x] + gain * residual[h, x]
                direction[h, x] = value
                smoothed[h, x] += value
                halo[r + 1, h, OWN, SELF, x] = value.astype(BF16)
                own_to_opposite(r + 1, h, x).start()
                if x % 2 == 1:
                    send_pair(r + 1, h, x - 1)

    def finish(r, h):
        @pl.when(r == ROUNDS - 2)
        def _():
            store_smoothed(h).start()

        @pl.when(r == ROUNDS - 1)
        def _():
            leaving[h] = restricted(h, 1 - parity).astype(BF16)
            hand_over(h).start()
            kept[h] = restricted(h, parity)
            store_kept(h).start()

    def half_step(t, last=True, older=True, newer=True):
        if last:
            rl, hl = lax.div(t - 2, HALVES), lax.rem(t, HALVES)
        if older:
            r, h = lax.div(t - 1, HALVES), lax.rem(t - 1, HALVES)
        if newer:
            rn, hn = lax.div(t, HALVES), lax.rem(t, HALVES)

        def pass_near(r, h, x):
            await_piece(r, h, NEAR, SELF, x, 1)
            near_to_ahead(r, h, x).start()
            if x % 2 == 1:
                near_to_sib(r, h, x - 1).start()

        def pass_far(x):
            await_piece(r, h, FAR, SELF, x, 1)
            far_to_sib(r, h, x).start()

        def far_blocks(row, sources):
            @pl.when((inner & has_far) if row == CROSS else has_far)
            def _():
                apply(r, h, FAR, row, sources)

        if older:
            pass_near(r, h, 3)

            @pl.when(inner)
            def _():
                for first in PAIRS:
                    await_piece(r, h, NEAR, CROSS, first, 2)
                    cross_to_ahead(r, h, first).start()

            apply(r, h, OWN, SELF)
        if last:
            await_piece(rl, hl, FAR, SIB, 3, 1)

            @pl.when(has_far)
            def _():
                apply(rl, hl, FAR, SIB, (3,))

            advance(rl, hl, (2, 3))
            finish(rl, hl)
        if older:
            await_pairs(r, h, OWN, SIB)
            apply(r, h, OWN, SIB)
            pass_far(0)
            apply(r, h, NEAR, SELF)

            @pl.when(inner)
            def _():
                await_pairs(r, h, OWN, CROSS)
                apply(r, h, OWN, CROSS)

            pass_far(1)
        if newer:
            pass_near(rn, hn, 0)
        if older:
            await_pairs(r, h, NEAR, SIB)
            apply(r, h, NEAR, SIB)

            @pl.when(inner)
            def _():
                apply(r, h, NEAR, CROSS)

            far_blocks(SELF, (0, 1))
            pass_far(2)
            for x in (0, 1):
                await_piece(r, h, FAR, SIB, x, 1)
            far_blocks(SIB, (0, 1))

            @pl.when(inner)
            def _():
                await_piece(r, h, FAR, CROSS, 0, 2)

            far_blocks(CROSS, (0, 1))
            advance(r, h, (0,))
        if older:
            pass_far(3)
        if newer:
            pass_near(rn, hn, 1)
            pass_near(rn, hn, 2)
        if older:
            far_blocks(SELF, (2, 3))

            @pl.when(inner)
            def _():
                await_piece(r, h, FAR, CROSS, 2, 2)

            far_blocks(CROSS, (2, 3))
            await_piece(r, h, FAR, SIB, 2, 1)
            far_blocks(SIB, (2,))
            advance(r, h, (1,))

    barrier = pltpu.get_barrier_semaphore()
    for device in (sibling, across, diagonal, opposite, ahead, behind):
        pl.semaphore_signal(barrier, inc=1, device_id=device, device_id_type=MESH)

    for h in range(HALVES):
        load_rhs[h].wait()

        def first_direction(x, carry):
            value = residual[h, x] / theta
            direction[h, x] = value
            smoothed[h, x] = value
            halo[0, h, OWN, SELF, x] = value.astype(BF16)
            return carry

        lax.fori_loop(0, xb, first_direction, 0)
        if h == HALVES - 1:
            for load in load_operator + [load_restrict]:
                load.start()
        if h == 0:
            pl.semaphore_wait(barrier, 6)
        for x in range(xb):
            own_to_opposite(0, h, x).start()
        for first in PAIRS:
            send_pair(0, h, first)

    load_codes.wait()
    shape = (columns.shape[0], slots)
    offset = lax.broadcasted_iota(jnp.int32, shape, 0)
    slot = lax.broadcasted_iota(jnp.int32, shape, 1)
    lane = lax.broadcasted_iota(jnp.int32, columns.shape, 1)
    table = jnp.zeros(columns.shape, jnp.int32)
    for x in range(xb):
        named = codes[pl.ds(x, 1), :]
        named = named + jnp.where(named >= slots // 2, 1, 0)
        found = jnp.min(jnp.where(named == offset, slot, slots), axis=1, keepdims=True)
        table = jnp.where(lane == x, found, table)
    columns[...] = table
    place_slots.start()

    steps = ROUNDS * HALVES
    half_step(0, last=False, older=False)
    for load in load_operator + [load_restrict, place_slots]:
        load.wait()
    half_step(1, last=False)

    def middle(t, carry):
        half_step(t)
        return carry

    lax.fori_loop(2, steps, middle, 0)
    half_step(steps, newer=False)
    half_step(steps + 1, older=False, newer=False)

    def drain(r, carry):
        for h in range(HALVES):
            for x in range(xb):
                own_to_opposite(r, h, x).wait_send()
                near_to_ahead(r, h, x).wait_send()
                far_to_sib(r, h, x).wait_send()
            for first in PAIRS:
                own_to_sib(r, h, first).wait_send()
                near_to_sib(r, h, first).wait_send()

        @pl.when(inner)
        def _():
            for h in range(HALVES):
                for first in PAIRS:
                    own_to_across(r, h, first).wait_send()
                    own_to_diagonal(r, h, first).wait_send()
                    cross_to_ahead(r, h, first).wait_send()

        return carry

    lax.fori_loop(0, ROUNDS, drain, 0)
    for h in range(HALVES):
        store_smoothed(h).wait()
        store_kept(h).wait()
        hand_over(h).wait()


def outputs_kernel(smoothed_in, kept_in, arrived_in, smoothed_out, coarse_out, smoothed, coarse, arrived, sem):
    load_arrived = pltpu.make_async_copy(arrived_in, arrived, sem.at[0])
    load_kept = pltpu.make_async_copy(kept_in, coarse, sem.at[1])
    store = pltpu.make_async_copy(coarse, coarse_out, sem.at[2])
    load_arrived.start()
    load_kept.start()
    blocks = range(smoothed.shape[0])
    loads = [pltpu.make_async_copy(smoothed_in.at[x], smoothed.at[x], sem.at[3 + 2 * x]) for x in blocks]
    stores = [pltpu.make_async_copy(smoothed.at[x], smoothed_out.at[x], sem.at[4 + 2 * x]) for x in blocks]
    for load in loads:
        load.start()
    load_arrived.wait()
    load_kept.wait()
    coarse[...] += jnp.concatenate([arrived[h] for h in range(HALVES)], axis=1).astype(F32)
    store.start()
    for x in blocks:
        loads[x].wait()
        stores[x].start()
    for x in blocks:
        stores[x].wait()
    store.wait()


def on_device(layers, rhs, blocks, diag_blocks, neighbours, bound, restrict_blocks, restrict_kind):
    xb, width, cols = rhs.shape[2:]
    slots = blocks.shape[3]
    half = cols // HALVES
    smem = pl.BlockSpec(memory_space=pltpu.SMEM)
    hbm = pl.BlockSpec(memory_space=pl.ANY)
    smoothed, kept, arrived = pl.pallas_call(
        functools.partial(smooth_kernel, layers),
        out_shape=(
            jax.ShapeDtypeStruct((xb, width, cols), F32),
            jax.ShapeDtypeStruct((width, cols), F32),
            jax.ShapeDtypeStruct((HALVES, width, half), BF16),
        ),
        in_specs=[smem, smem, hbm, hbm, hbm, hbm, hbm],
        out_specs=(hbm, hbm, hbm),
        scratch_shapes=[
            pltpu.VMEM((xb, slots + 1, width, width), BF16),
            pltpu.VMEM((ROUNDS, HALVES, 3, 3, xb, width, half), BF16),
            pltpu.VMEM((HALVES, xb, width, half), F32),
            pltpu.VMEM((HALVES, xb, width, half), F32),
            pltpu.VMEM((HALVES, xb, width, half), F32),
            pltpu.VMEM(restrict_blocks.shape, BF16),
            pltpu.VMEM((HALVES, width, half), F32),
            pltpu.VMEM((HALVES, width, half), BF16),
            pltpu.VMEM((xb, slots), jnp.int32),
            pltpu.VMEM((32, 128), jnp.int32),
            pltpu.SMEM((32, 128), jnp.int32),
            pltpu.SemaphoreType.DMA((6 + xb,)),
            pltpu.SemaphoreType.DMA((2, HALVES)),
            pltpu.SemaphoreType.DMA((ROUNDS, HALVES, 8, xb)),
            pltpu.SemaphoreType.DMA((ROUNDS, HALVES, 9, xb)),
            pltpu.SemaphoreType.DMA((2, HALVES)),
        ],
        compiler_params=pltpu.CompilerParams(
            collective_id=0, has_side_effects=True, vmem_limit_bytes=56 * 2**20
        ),
        cost_estimate=pl.CostEstimate(flops=6 * 10**9, bytes_accessed=11 * 10**6, transcendentals=0),
        name="smooth_and_restrict",
    )(restrict_kind[0, 0], bound, neighbours[0, 0], rhs[0, 0], blocks[0, 0], diag_blocks[0, 0], restrict_blocks)
    smoothed, coarse = pl.pallas_call(
        outputs_kernel,
        out_shape=(
            jax.ShapeDtypeStruct((xb, width, cols), F32),
            jax.ShapeDtypeStruct((width, cols), F32),
        ),
        in_specs=[hbm, hbm, hbm],
        out_specs=(hbm, hbm),
        scratch_shapes=[
            pltpu.VMEM((xb, width, cols), F32),
            pltpu.VMEM((width, cols), F32),
            pltpu.VMEM((HALVES, width, half), BF16),
            pltpu.SemaphoreType.DMA((3 + 2 * xb,)),
        ],
        compiler_params=pltpu.CompilerParams(vmem_limit_bytes=56 * 2**20),
        name="outputs",
    )(smoothed, kept, arrived)
    return smoothed[None, None], coarse[None, None, None]


def solution(mesh):
    return jax.shard_map(
        functools.partial(on_device, mesh.shape["slab"]),
        mesh=mesh,
        in_specs=(
            P("slab", "quad", None, None, None),
            P("slab", "quad", None, None, None, None),
            P("slab", "quad", None, None, None),
            P("slab", "quad", None, None),
            P(),
            P(),
            P("slab", "quad", None),
        ),
        out_specs=(P("slab", "quad", None, None, None), P("slab", "quad", None, None, None)),
        check_vma=False,
    )
```

```python
import functools

import jax
import jax.numpy as jnp
from jax import lax
from jax.experimental import pallas as pl
from jax.experimental.pallas import tpu as pltpu
from jax.sharding import PartitionSpec as P

OWN, NEAR, FAR = 0, 1, 2
SELF, SIB, CROSS = 0, 1, 2
ROUNDS = 3
HALVES = 2
PAIRS = (0, 2)
MESH = pl.DeviceIdType.MESH
F32 = jnp.float32
BF16 = jnp.bfloat16


def smooth_kernel(
    layers,
    kind_ref,
    bound_ref,
    code_hbm,
    rhs_hbm,
    blocks_hbm,
    diag_hbm,
    restrict_hbm,
    smoothed_hbm,
    kept_hbm,
    arrived_hbm,
    oper,
    halo,
    residual,
    direction,
    smoothed,
    restrict,
    kept,
    leaving,
    codes,
    columns,
    slot_ref,
    load_sem,
    store_sem,
    send_sem,
    recv_sem,
    coarse_sem,
):
    s = lax.axis_index("slab")
    q = lax.axis_index("quad")
    parity = lax.rem(s, 2)
    inner = (q == 1) | (q == 2)
    near_s = s + 1 - 2 * parity
    step = 2 - 4 * parity
    sibling = (s, q + 1 - 2 * lax.rem(q, 2))
    across = (s, 3 - q)
    diagonal = (near_s, 3 - q)
    opposite = (near_s, q)
    ahead = (lax.rem(s + step + layers, layers), q)
    behind = (lax.rem(s - step + layers, layers), q)
    dz_near = 2 - 2 * parity
    dy_sib = 2 - 2 * lax.rem(q, 2)
    has_far = jnp.where(parity == 0, s > 0, s < layers - 1)
    xb, width, half = residual.shape[1:]
    slots = blocks_hbm.shape[1]

    load_rhs = [
        pltpu.make_async_copy(rhs_hbm.at[:, :, pl.ds(h * half, half)], residual.at[h], load_sem.at[h])
        for h in range(HALVES)
    ]
    load_operator = [pltpu.make_async_copy(diag_hbm, oper.at[:, slots], load_sem.at[2])] + [
        pltpu.make_async_copy(blocks_hbm.at[x], oper.at[x, pl.ds(0, slots)], load_sem.at[3 + x]) for x in range(xb)
    ]
    load_restrict = pltpu.make_async_copy(restrict_hbm, restrict, load_sem.at[3 + xb])
    load_codes = pltpu.make_async_copy(code_hbm, codes, load_sem.at[4 + xb])
    place_slots = pltpu.make_async_copy(columns, slot_ref, load_sem.at[5 + xb])
    load_codes.start()
    for load in load_rhs:
        load.start()

    def copy(r, h, lane, src, dst, device, first, count):
        blocks = pl.ds(first, count)
        return pltpu.make_async_remote_copy(
            src_ref=halo.at[r, h, src[0], src[1], blocks],
            dst_ref=halo.at[r, h, dst[0], dst[1], blocks],
            send_sem=send_sem.at[r, h, lane, first],
            recv_sem=recv_sem.at[r, h, dst[0] * 3 + dst[1], first],
            device_id=device,
            device_id_type=MESH,
        )

    def own_to_sib(r, h, first):
        return copy(r, h, 0, (OWN, SELF), (OWN, SIB), sibling, first, 2)

    def own_to_across(r, h, first):
        return copy(r, h, 1, (OWN, SELF), (OWN, CROSS), across, first, 2)

    def own_to_diagonal(r, h, first):
        return copy(r, h, 2, (OWN, SELF), (NEAR, CROSS), diagonal, first, 2)

    def own_to_opposite(r, h, first):
        return copy(r, h, 3, (OWN, SELF), (NEAR, SELF), opposite, first, 1)

    def near_to_sib(r, h, first):
        return copy(r, h, 4, (NEAR, SELF), (NEAR, SIB), sibling, first, 2)

    def near_to_ahead(r, h, first):
        return copy(r, h, 5, (NEAR, SELF), (FAR, SELF), ahead, first, 1)

    def cross_to_ahead(r, h, first):
        return copy(r, h, 6, (NEAR, CROSS), (FAR, CROSS), ahead, first, 2)

    def far_to_sib(r, h, first):
        return copy(r, h, 7, (FAR, SELF), (FAR, SIB), sibling, first, 1)

    def await_piece(r, h, a, b, first, count):
        copy(r, h, 0, (a, b), (a, b), sibling, first, count).wait_recv()

    def await_pairs(r, h, a, b):
        for first in PAIRS:
            await_piece(r, h, a, b, first, 2)

    def send_pair(r, h, first):
        @pl.when(inner)
        def _():
            own_to_diagonal(r, h, first).start()

        own_to_sib(r, h, first).start()

        @pl.when(inner)
        def _():
            own_to_across(r, h, first).start()

    def apply(r, h, a, b, sources=range(4)):
        dz = (1, dz_near, 2 - dz_near)[a]
        dy = (1, dy_sib, 2 - dy_sib)[b]
        base = dz * 9 + dy * 3
        for source in sources:
            targets = [x for x in (source - 1, source, source + 1) if 0 <= x < xb]
            rows = [oper[x, slot_ref[base + source - x + 1, x]] for x in targets]
            moved = jnp.dot(jnp.concatenate(rows, axis=0), halo[r, h, a, b, source], preferred_element_type=F32)
            for i, x in enumerate(targets):
                residual[h, x] -= moved[i * width : (i + 1) * width]

    bound = bound_ref[0]
    sigma = 9.0 / 7.0
    theta = 9.0 * bound / 16.0
    delta = 7.0 * bound / 16.0
    rho_0 = 1.0 / sigma
    rho_1 = 1.0 / (2.0 * sigma - rho_0)
    rho_2 = 1.0 / (2.0 * sigma - rho_1)

    def hand_over(h):
        return pltpu.make_async_remote_copy(
            src_ref=leaving.at[h],
            dst_ref=arrived_hbm.at[h],
            send_sem=coarse_sem.at[0, h],
            recv_sem=coarse_sem.at[1, h],
            device_id=opposite,
            device_id_type=MESH,
        )

    def store_smoothed(h):
        return pltpu.make_async_copy(
            smoothed.at[h], smoothed_hbm.at[:, :, pl.ds(pl.multiple_of(h * half, half), half)], store_sem.at[0, h]
        )

    def store_kept(h):
        return pltpu.make_async_copy(
            kept.at[h], kept_hbm.at[:, pl.ds(pl.multiple_of(h * half, half), half)], store_sem.at[1, h]
        )

    def restricted(h, pair):
        total = None
        for i in range(2):
            x = 2 * pair + i
            term = jnp.dot(restrict[kind_ref[x]], residual[h, x].astype(BF16), preferred_element_type=F32)
            total = term if total is None else total + term
        return total

    def advance(r, h, targets):
        @pl.when(r < ROUNDS - 1)
        def _():
            first = r == 0
            scale = jnp.where(first, rho_1 * rho_0, rho_2 * rho_1)
            gain = jnp.where(first, 2.0 * rho_1 / delta, 2.0 * rho_2 / delta)
            for x in targets:
                value = scale * direction[h, x] + gain * residual[h, x]
                direction[h, x] = value
                smoothed[h, x] += value
                halo[r + 1, h, OWN, SELF, x] = value.astype(BF16)
                own_to_opposite(r + 1, h, x).start()
                if x % 2 == 1:
                    send_pair(r + 1, h, x - 1)

    def finish(r, h):
        @pl.when(r == ROUNDS - 2)
        def _():
            store_smoothed(h).start()

        @pl.when(r == ROUNDS - 1)
        def _():
            leaving[h] = restricted(h, 1 - parity).astype(BF16)
            hand_over(h).start()
            kept[h] = restricted(h, parity)
            store_kept(h).start()

    def half_step(t, last=True, older=True, newer=True):
        if last:
            rl, hl = lax.div(t - 2, HALVES), lax.rem(t, HALVES)
        if older:
            r, h = lax.div(t - 1, HALVES), lax.rem(t - 1, HALVES)
        if newer:
            rn, hn = lax.div(t, HALVES), lax.rem(t, HALVES)

        def pass_near(r, h, x):
            await_piece(r, h, NEAR, SELF, x, 1)
            near_to_ahead(r, h, x).start()
            if x % 2 == 1:
                near_to_sib(r, h, x - 1).start()

        def pass_far(x):
            await_piece(r, h, FAR, SELF, x, 1)
            far_to_sib(r, h, x).start()

        def far_blocks(row, sources):
            @pl.when((inner & has_far) if row == CROSS else has_far)
            def _():
                apply(r, h, FAR, row, sources)

        if older:
            pass_near(r, h, 3)

            @pl.when(inner)
            def _():
                for first in PAIRS:
                    await_piece(r, h, NEAR, CROSS, first, 2)
                    cross_to_ahead(r, h, first).start()

        if last:
            await_piece(rl, hl, FAR, SIB, 3, 1)

            @pl.when(has_far)
            def _():
                apply(rl, hl, FAR, SIB, (3,))

            advance(rl, hl, (2, 3))
            finish(rl, hl)
        if older:
            apply(r, h, OWN, SELF)
            await_pairs(r, h, OWN, SIB)
            apply(r, h, OWN, SIB)
            pass_far(0)
            apply(r, h, NEAR, SELF)

            @pl.when(inner)
            def _():
                await_pairs(r, h, OWN, CROSS)
                apply(r, h, OWN, CROSS)

            pass_far(1)
        if newer:
            pass_near(rn, hn, 0)
        if older:
            await_pairs(r, h, NEAR, SIB)
            apply(r, h, NEAR, SIB)

            @pl.when(inner)
            def _():
                apply(r, h, NEAR, CROSS)

            far_blocks(SELF, (0, 1))
            pass_far(2)
            for x in (0, 1):
                await_piece(r, h, FAR, SIB, x, 1)
            far_blocks(SIB, (0, 1))

            @pl.when(inner)
            def _():
                await_piece(r, h, FAR, CROSS, 0, 2)

            far_blocks(CROSS, (0, 1))
            advance(r, h, (0,))
        if older:
            pass_far(3)
        if newer:
            pass_near(rn, hn, 1)
            pass_near(rn, hn, 2)
        if older:
            far_blocks(SELF, (2,))

            @pl.when(inner)
            def _():
                await_piece(r, h, FAR, CROSS, 2, 2)

            far_blocks(CROSS, (2,))
            await_piece(r, h, FAR, SIB, 2, 1)
            far_blocks(SIB, (2,))
            advance(r, h, (1,))
            far_blocks(SELF, (3,))
            far_blocks(CROSS, (3,))

    barrier = pltpu.get_barrier_semaphore()
    for device in (sibling, across, diagonal, opposite, ahead, behind):
        pl.semaphore_signal(barrier, inc=1, device_id=device, device_id_type=MESH)

    for h in range(HALVES):
        load_rhs[h].wait()

        def first_direction(x, carry):
            value = residual[h, x] / theta
            direction[h, x] = value
            smoothed[h, x] = value
            halo[0, h, OWN, SELF, x] = value.astype(BF16)
            return carry

        lax.fori_loop(0, xb, first_direction, 0)
        if h == HALVES - 1:
            for load in load_operator + [load_restrict]:
                load.start()
        if h == 0:
            pl.semaphore_wait(barrier, 6)
        for x in range(xb):
            own_to_opposite(0, h, x).start()
        for first in PAIRS:
            send_pair(0, h, first)

    load_codes.wait()
    shape = (columns.shape[0], slots)
    offset = lax.broadcasted_iota(jnp.int32, shape, 0)
    slot = lax.broadcasted_iota(jnp.int32, shape, 1)
    lane = lax.broadcasted_iota(jnp.int32, columns.shape, 1)
    table = jnp.zeros(columns.shape, jnp.int32)
    for x in range(xb):
        named = codes[pl.ds(x, 1), :]
        named = named + jnp.where(named >= slots // 2, 1, 0)
        found = jnp.min(jnp.where(named == offset, slot, slots), axis=1, keepdims=True)
        table = jnp.where(lane == x, found, table)
    columns[...] = table
    place_slots.start()

    steps = ROUNDS * HALVES
    half_step(0, last=False, older=False)
    for load in load_operator + [load_restrict, place_slots]:
        load.wait()
    half_step(1, last=False)

    def middle(t, carry):
        half_step(t)
        return carry

    lax.fori_loop(2, steps, middle, 0)
    half_step(steps, newer=False)
    half_step(steps + 1, older=False, newer=False)

    def drain(r, carry):
        for h in range(HALVES):
            for x in range(xb):
                own_to_opposite(r, h, x).wait_send()
                near_to_ahead(r, h, x).wait_send()
                far_to_sib(r, h, x).wait_send()
            for first in PAIRS:
                own_to_sib(r, h, first).wait_send()
                near_to_sib(r, h, first).wait_send()

        @pl.when(inner)
        def _():
            for h in range(HALVES):
                for first in PAIRS:
                    own_to_across(r, h, first).wait_send()
                    own_to_diagonal(r, h, first).wait_send()
                    cross_to_ahead(r, h, first).wait_send()

        return carry

    lax.fori_loop(0, ROUNDS, drain, 0)
    for h in range(HALVES):
        store_smoothed(h).wait()
        store_kept(h).wait()
        hand_over(h).wait()


def outputs_kernel(smoothed_in, kept_in, arrived_in, smoothed_out, coarse_out, smoothed, coarse, arrived, sem):
    load_arrived = pltpu.make_async_copy(arrived_in, arrived, sem.at[0])
    load_kept = pltpu.make_async_copy(kept_in, coarse, sem.at[1])
    store = pltpu.make_async_copy(coarse, coarse_out, sem.at[2])
    load_arrived.start()
    load_kept.start()
    blocks = range(smoothed.shape[0])
    loads = [pltpu.make_async_copy(smoothed_in.at[x], smoothed.at[x], sem.at[3 + 2 * x]) for x in blocks]
    stores = [pltpu.make_async_copy(smoothed.at[x], smoothed_out.at[x], sem.at[4 + 2 * x]) for x in blocks]
    for load in loads:
        load.start()
    load_arrived.wait()
    load_kept.wait()
    coarse[...] += jnp.concatenate([arrived[h] for h in range(HALVES)], axis=1).astype(F32)
    store.start()
    for x in blocks:
        loads[x].wait()
        stores[x].start()
    for x in blocks:
        stores[x].wait()
    store.wait()


def on_device(layers, rhs, blocks, diag_blocks, neighbours, bound, restrict_blocks, restrict_kind):
    xb, width, cols = rhs.shape[2:]
    slots = blocks.shape[3]
    half = cols // HALVES
    smem = pl.BlockSpec(memory_space=pltpu.SMEM)
    hbm = pl.BlockSpec(memory_space=pl.ANY)
    smoothed, kept, arrived = pl.pallas_call(
        functools.partial(smooth_kernel, layers),
        out_shape=(
            jax.ShapeDtypeStruct((xb, width, cols), F32),
            jax.ShapeDtypeStruct((width, cols), F32),
            jax.ShapeDtypeStruct((HALVES, width, half), BF16),
        ),
        in_specs=[smem, smem, hbm, hbm, hbm, hbm, hbm],
        out_specs=(hbm, hbm, hbm),
        scratch_shapes=[
            pltpu.VMEM((xb, slots + 1, width, width), BF16),
            pltpu.VMEM((ROUNDS, HALVES, 3, 3, xb, width, half), BF16),
            pltpu.VMEM((HALVES, xb, width, half), F32),
            pltpu.VMEM((HALVES, xb, width, half), F32),
            pltpu.VMEM((HALVES, xb, width, half), F32),
            pltpu.VMEM(restrict_blocks.shape, BF16),
            pltpu.VMEM((HALVES, width, half), F32),
            pltpu.VMEM((HALVES, width, half), BF16),
            pltpu.VMEM((xb, slots), jnp.int32),
            pltpu.VMEM((32, 128), jnp.int32),
            pltpu.SMEM((32, 128), jnp.int32),
            pltpu.SemaphoreType.DMA((6 + xb,)),
            pltpu.SemaphoreType.DMA((2, HALVES)),
            pltpu.SemaphoreType.DMA((ROUNDS, HALVES, 8, xb)),
            pltpu.SemaphoreType.DMA((ROUNDS, HALVES, 9, xb)),
            pltpu.SemaphoreType.DMA((2, HALVES)),
        ],
        compiler_params=pltpu.CompilerParams(
            collective_id=0, has_side_effects=True, vmem_limit_bytes=56 * 2**20
        ),
        cost_estimate=pl.CostEstimate(flops=6 * 10**9, bytes_accessed=11 * 10**6, transcendentals=0),
        name="smooth_and_restrict",
    )(restrict_kind[0, 0], bound, neighbours[0, 0], rhs[0, 0], blocks[0, 0], diag_blocks[0, 0], restrict_blocks)
    smoothed, coarse = pl.pallas_call(
        outputs_kernel,
        out_shape=(
            jax.ShapeDtypeStruct((xb, width, cols), F32),
            jax.ShapeDtypeStruct((width, cols), F32),
        ),
        in_specs=[hbm, hbm, hbm],
        out_specs=(hbm, hbm),
        scratch_shapes=[
            pltpu.VMEM((xb, width, cols), F32),
            pltpu.VMEM((width, cols), F32),
            pltpu.VMEM((HALVES, width, half), BF16),
            pltpu.SemaphoreType.DMA((3 + 2 * xb,)),
        ],
        compiler_params=pltpu.CompilerParams(vmem_limit_bytes=56 * 2**20),
        name="outputs",
    )(smoothed, kept, arrived)
    return smoothed[None, None], coarse[None, None, None]


def solution(mesh):
    return jax.shard_map(
        functools.partial(on_device, mesh.shape["slab"]),
        mesh=mesh,
        in_specs=(
            P("slab", "quad", None, None, None),
            P("slab", "quad", None, None, None, None),
            P("slab", "quad", None, None, None),
            P("slab", "quad", None, None),
            P(),
            P(),
            P("slab", "quad", None),
        ),
        out_specs=(P("slab", "quad", None, None, None), P("slab", "quad", None, None, None)),
        check_vma=False,
    )
```
